512 devices in a mesh: dp: 32 (over z, x), seq: 16 (over y, core).
Axes of the slice: x: 4, y: 8, z: 8, core: 2. Of those that a mesh axis runs over, the one named last changes fastest.
Arguments:
- queries: bfloat16 [32, 16, 224, 1536], P('dp', 'seq')
- key_rows: bfloat16 [32, 16, 224, 1536], P('dp', 'seq')
- values: bfloat16 [32, 16, 224, 1536], P('dp', 'seq'), may hold values from -6 to 6
- cotangent: bfloat16 [32, 16, 224, 1536], P('dp', 'seq')
- frame_counts: int32 [32], replicated, may hold values from 2 to 16, as said below
- position_counts: int32 [32], replicated, may hold values from 56 to 224, as said below
- head_scale: float32 [12], replicated, may hold values from 0.5 to 2
- frame_slope: float32 [12], replicated, may hold values from 0.02 to 0.5
Outputs:
- grad_queries: bfloat16 [32, 16, 224, 1536], P('dp', 'seq')
- grad_keys: bfloat16 [32, 16, 224, 1536], P('dp', 'seq')
- grad_values: bfloat16 [32, 16, 224, 1536], P('dp', 'seq')
- grad_scale: float32 [12], replicated
- grad_slope: float32 [12], replicated
The draws below stay inside these ranges and needn't reach their ends.
Inputs may be any that keep to these rules, and one draw needn't show every extreme that they name: `frame_counts`: frames in use of each clip, the others are padding; some clip uses all 16. `position_counts`: spatial tokens in use in each frame of a clip, the others are padding; some clip uses all 224.
All inputs are finite; a program needn't handle non-finite values.
Results may differ from the reference program's by a relative error of at most 0.0063.
Values may be sent and summed in bfloat16 or wider, within the bound.
No kernel may reach another device: no remote copies, remote signals or barrier semaphores. Data moves between devices by JAX's collectives and lax.ppermute only.
A program may use at most 64 MiB of HBM per device.

```python
import math
import jax
import jax.numpy as jnp
from jax import lax

H = 12
C = 1536
S = 224
F = 16
N_DP = 32


def draw_queries(key, part):
    key = jax.random.fold_in(key, 1)
    shape = (N_DP, F, S, C)
    base = jax.random.normal(key, shape, jnp.float32)
    return base.astype(jnp.bfloat16)


def draw_key_rows(key, part):
    key = jax.random.fold_in(key, 2)
    shape = (N_DP, F, S, C)
    base = jax.random.normal(key, shape, jnp.float32)
    return base.astype(jnp.bfloat16)


def draw_cotangent(key, part):
    key = jax.random.fold_in(key, 3)
    shape = (N_DP, F, S, C)
    order = (jnp.arange(N_DP)[:, None] * F + jnp.arange(F)[None, :]).astype(jnp.float32)
    ramp = 1.0 + 2.0 * order / (N_DP * F - 1)
    base = jax.random.normal(key, shape, jnp.float32)
    return (base * ramp[:, :, None, None]).astype(jnp.bfloat16)


def draw_frame_counts(key, part):
    key = jax.random.fold_in(key, 4)
    counts = jax.random.randint(key, (N_DP,), 2, F + 1)
    fullest = jax.random.randint(jax.random.fold_in(key, 5), (), 0, N_DP)
    return counts.at[fullest].set(F).astype(jnp.int32)


def draw_position_counts(key, part):
    key = jax.random.fold_in(key, 6)
    counts = jax.random.randint(key, (N_DP,), S // 4, S + 1)
    fullest = jax.random.randint(jax.random.fold_in(key, 7), (), 0, N_DP)
    return counts.at[fullest].set(S).astype(jnp.int32)


def steps_of(rng, shape, split, least, high):
    gain = 1.0
    for dim, blocks in split:
        heights = jax.random.uniform(jax.random.fold_in(jax.random.fold_in(rng, 6), dim), (blocks,), jnp.float32, least / len(split), high / len(split))
        gain = gain * jnp.repeat(jnp.exp(heights), shape[dim] // blocks).reshape((-1,) + (1,) * (len(shape) - 1 - dim))
    return gain


def bell_draw(rng, dims, width, most, pieces=(), held_as=jnp.bfloat16):
    entries = jax.random.normal(rng, dims, jnp.float32) * width
    if len(pieces) > 0:
        entries = steps_of(rng, dims, pieces, -0.22, 0.18) * entries
    return jnp.clip(entries, min=-most, max=most).astype(held_as)


def setup_inputs(seed: int = 0) -> dict:
    key_list = jax.random.split(jax.random.key(seed), 9)
    return {
        "queries": draw_queries(jax.random.fold_in(key_list[8], 71), 0),
        "key_rows": draw_key_rows(jax.random.fold_in(key_list[8], 71), 0),
        "values": bell_draw(key_list[2], (N_DP, F, S, C), 1.0, 6.0, ((0, 32), (1, 16))),
        "cotangent": draw_cotangent(jax.random.fold_in(key_list[8], 71), 0),
        "frame_counts": draw_frame_counts(jax.random.fold_in(key_list[8], 71), 0),
        "position_counts": draw_position_counts(jax.random.fold_in(key_list[8], 71), 0),
        "head_scale": jnp.clip(jnp.exp(jax.random.uniform(key_list[6], (H,), jnp.float32, math.log(0.5), math.log(2.0))), 0.5, 2.0),
        "frame_slope": jnp.clip(jnp.exp(jax.random.uniform(key_list[7], (H,), jnp.float32, math.log(0.02), math.log(0.5))), 0.02, 0.5),
    }


def attend(queries, key_rows, values, grad_out, scale, coef, distance, key_live, token_form):
    key_form = token_form.replace('l', 'm')
    head_size = queries.shape[-1]
    factor = scale / math.sqrt(head_size)
    query_f = queries.astype(jnp.float32)
    key_f = key_rows.astype(jnp.float32)
    value_f = values.astype(jnp.float32)
    grad_f = grad_out.astype(jnp.float32)
    raw_scores = jnp.einsum(token_form + ',' + key_form + '->bhlm', query_f, key_f)
    scores = raw_scores * factor[:, None, None] - coef[:, None, None] * distance
    scores = jnp.where(key_live, scores, -jnp.inf)
    row_top = lax.optimization_barrier(jnp.max(scores, axis=-1, keepdims=True))
    exponent = jnp.exp(scores - row_top)
    probability = exponent / lax.optimization_barrier(jnp.sum(exponent, axis=-1, keepdims=True))
    weights = probability.astype(jnp.bfloat16).astype(jnp.float32)
    grad_probs = jnp.einsum(token_form + ',' + key_form + '->bhlm', grad_f, value_f)
    grad_values = jnp.einsum('bhlm,' + token_form + '->' + key_form, weights, grad_f)
    grad_scores = probability * (grad_probs - lax.optimization_barrier(jnp.sum(probability * grad_probs, axis=-1, keepdims=True)))
    rounded = grad_scores.astype(jnp.bfloat16).astype(jnp.float32)
    grad_queries = jnp.einsum('bhlm,' + key_form + '->' + token_form, rounded, key_f) * factor[:, None]
    grad_keys = jnp.einsum('bhlm,' + token_form + '->' + key_form, rounded, query_f) * factor[:, None]
    scale_terms = lax.optimization_barrier(jnp.sum(grad_scores * raw_scores, axis=(2, 3))) / math.sqrt(head_size)
    slope_terms = -lax.optimization_barrier(jnp.sum(grad_scores * distance, axis=(2, 3)))
    return (grad_queries, grad_keys, grad_values, scale_terms, slope_terms)

def one_clip(queries, key_rows, values, cotangent, frame_count, position_count, head_scale, frame_slope):
    frames_all = queries.shape[0]
    spatial = queries.shape[1]
    heads = head_scale.shape[0]
    head_size = queries.shape[2] // heads
    shape_four = (frames_all, spatial, heads, head_size)
    query_four = queries.reshape(shape_four)
    key_four = key_rows.reshape(shape_four)
    value_four = values.reshape(shape_four)
    cot_four = cotangent.reshape(shape_four)
    frame_live = jnp.arange(frames_all) < frame_count
    place_live = jnp.arange(spatial) < position_count
    live = frame_live[:, None] & place_live[None, :]
    masked = jnp.where(live[:, :, None, None], cot_four, jnp.zeros((), cot_four.dtype))
    zero_heads = jnp.zeros_like(frame_slope)
    flat_space = jnp.zeros((spatial, spatial), frame_slope.dtype)
    space_grads = attend(query_four, key_four, value_four, masked, head_scale, zero_heads, flat_space, place_live, 'blhd')
    frame_iota = jnp.arange(frames_all)
    steps_apart = jnp.abs(frame_iota[:, None] - frame_iota[None, :]).astype(frame_slope.dtype)
    time_grads = attend(query_four, key_four, value_four, masked, head_scale, frame_slope, steps_apart, frame_live, 'lbhd')
    results = []
    for index in range(3):
        sent = lax.optimization_barrier(time_grads[index].astype(jnp.bfloat16))
        total = space_grads[index] + sent.astype(jnp.float32)
        results.append(total.astype(jnp.bfloat16).reshape(frames_all, spatial, heads * head_size))
    scale_grad = lax.optimization_barrier(jnp.sum(space_grads[3], axis=0)) + lax.optimization_barrier(jnp.sum(time_grads[3], axis=0))
    slope_grad = lax.optimization_barrier(jnp.sum(time_grads[4], axis=0))
    return (results[0], results[1], results[2], scale_grad, slope_grad)

def reference(queries, key_rows, values, cotangent, frame_counts, position_counts, head_scale, frame_slope):

    def per_clip(items):
        return one_clip(items[0], items[1], items[2], items[3], items[4], items[5], head_scale, frame_slope)
    outputs = lax.map(per_clip, (queries, key_rows, values, cotangent, frame_counts, position_counts))
    return (outputs[0], outputs[1], outputs[2], lax.optimization_barrier(jnp.sum(outputs[3], axis=0)), lax.optimization_barrier(jnp.sum(outputs[4], axis=0)))
```

```python
import functools
import math

import jax
import jax.numpy as jnp
from jax import lax
from jax.experimental import pallas as pl
from jax.experimental.pallas import tpu as pltpu
from jax.sharding import PartitionSpec as P

HEAD = 128
ROW_SPLIT = 4
HEAD_SPLIT = 4
STEP = 8
BATCH = 7
SCOPED = 32 * 2**20
STREAM = 60 * 2**20


def dot(a, b, dims):
    return lax.dot_general(a, b, (dims, ((), ())), preferred_element_type=jnp.float32)


AB_T = ((1,), (1,))
AB = ((1,), (0,))
A_TB = ((0,), (0,))


def live_rows(fc_ref, pc_ref, shape):
    clip = lax.axis_index("dp")
    positions = jnp.where(lax.axis_index("seq") < fc_ref[clip], pc_ref[clip], 0)
    return lax.broadcasted_iota(jnp.int32, shape, 0) < positions


def pack_kernel(
    fc_ref, pc_ref, q_hbm, k_hbm, v_hbm, g_hbm, out_hbm, held_ref, out_ref, in_sem, out_sem
):
    spatial = held_ref.shape[1]
    rows, half = spatial // ROW_SPLIT, spatial // 2
    heads = out_ref.shape[1]
    width = heads * HEAD
    targets = out_ref.shape[0] // 2

    def fetch(index, part):
        here = pl.ds(part * half, half)
        return pltpu.make_async_copy(
            (q_hbm, k_hbm, v_hbm, g_hbm)[index].at[here], held_ref.at[index, here], in_sem.at[part, index]
        )

    def send(part):
        here = pl.ds(part * targets, targets)
        return pltpu.make_async_copy(out_ref.at[here], out_hbm.at[here], out_sem.at[part])

    for part in range(2):
        for index in range(4):
            fetch(index, part).start()
    live = live_rows(fc_ref, pc_ref, (spatial, width))
    for part in range(2):
        for index in range(4):
            fetch(index, part).wait()
            for group in range(HEAD_SPLIT):
                value = held_ref[index, pl.ds(part * half, half), pl.ds(group * width, width)]
                if index == 3:
                    value = jnp.where(live[part * half : (part + 1) * half], value, 0)
                    value = value.astype(jnp.bfloat16)
                for step in range(ROW_SPLIT // 2):
                    target = (part * (ROW_SPLIT // 2) + step) * HEAD_SPLIT + group
                    for head in range(heads):
                        out_ref[target, head, pl.ds(index * rows, rows), :] = value[
                            step * rows : (step + 1) * rows, head * HEAD : (head + 1) * HEAD
                        ]
        send(part).start()
    for part in range(2):
        send(part).wait()


def pack(frame_counts, position_counts, arrays):
    spatial, channels = arrays[0].shape
    rows = spatial // ROW_SPLIT
    smem = pl.BlockSpec(memory_space=pltpu.SMEM)
    hbm = pl.BlockSpec(memory_space=pltpu.HBM)
    shape = (ROW_SPLIT * HEAD_SPLIT, channels // (HEAD * HEAD_SPLIT), 4 * rows, HEAD)
    return pl.pallas_call(
        pack_kernel,
        in_specs=[smem] * 2 + [hbm] * 4,
        out_specs=hbm,
        out_shape=jax.ShapeDtypeStruct(shape, jnp.bfloat16),
        scratch_shapes=[
            pltpu.VMEM((4, spatial, channels), jnp.bfloat16),
            pltpu.VMEM(shape, jnp.bfloat16),
            pltpu.SemaphoreType.DMA((2, 4)),
            pltpu.SemaphoreType.DMA((2,)),
        ],
        compiler_params=pltpu.CompilerParams(vmem_limit_bytes=STREAM),
        cost_estimate=pl.CostEstimate(
            flops=0, bytes_accessed=4 * 4 * spatial * channels, transcendentals=0
        ),
        name="pack",
    )(frame_counts, position_counts, *arrays)


def space_kernel(
    fc_ref, pc_ref, scale_ref, q_ref, k_ref, v_ref, g_ref, dq_ref, dk_ref, dv_ref, sum_ref
):
    head = pl.program_id(0)
    factor = scale_ref[head] * (1.0 / math.sqrt(HEAD))
    query, key, value = q_ref[...], k_ref[...], v_ref[...]
    grad = g_ref[...]
    grad = jnp.where(live_rows(fc_ref, pc_ref, grad.shape), grad, 0).astype(grad.dtype)
    raw = dot(key, query, AB_T)
    key_row = lax.broadcasted_iota(jnp.int32, raw.shape, 0)
    live = key_row < pc_ref[lax.axis_index("dp")]
    scores = jnp.where(live, raw * factor, -jnp.inf)
    exponent = jnp.exp(scores - jnp.max(scores, axis=0, keepdims=True))
    prob = exponent * (1.0 / jnp.sum(exponent, axis=0, keepdims=True))
    grad_prob = dot(value, grad, AB_T)
    weighted = prob * grad_prob
    grad_score = weighted - prob * jnp.sum(weighted, axis=0, keepdims=True)
    rounded = grad_score.astype(jnp.bfloat16)
    dq_ref[...] = dot(rounded, key, A_TB) * factor
    dk_ref[...] = dot(rounded, query, AB) * factor
    dv_ref[...] = dot(prob.astype(jnp.bfloat16), grad, AB)
    term = jnp.sum(grad_score * raw) * (1.0 / math.sqrt(HEAD))
    lane = lax.broadcasted_iota(jnp.int32, sum_ref.shape, 1)

    @pl.when(head == 0)
    def _():
        sum_ref[...] = jnp.zeros_like(sum_ref)

    sum_ref[...] += jnp.where(lane == head, term, 0.0)


def space(frame_counts, position_counts, head_scale, arrays):
    spatial, channels = arrays[0].shape
    heads = channels // HEAD
    smem = pl.BlockSpec(memory_space=pltpu.SMEM)
    block = pl.BlockSpec((spatial, HEAD), lambda i: (0, i))
    return pl.pallas_call(
        space_kernel,
        grid=(heads,),
        in_specs=[smem] * 3 + [block] * 4,
        out_specs=[block] * 3 + [pl.BlockSpec((1, HEAD), lambda i: (0, 0))],
        out_shape=[jax.ShapeDtypeStruct((spatial, channels), jnp.float32)] * 3
        + [jax.ShapeDtypeStruct((1, HEAD), jnp.float32)],
        compiler_params=pltpu.CompilerParams(vmem_limit_bytes=SCOPED),
        cost_estimate=pl.CostEstimate(
            flops=10 * heads * spatial * spatial * HEAD,
            bytes_accessed=20 * spatial * channels,
            transcendentals=heads * spatial * spatial,
        ),
        name="space",
    )(frame_counts, position_counts, head_scale, *arrays)


def time_kernel(
    fc_ref, scale_ref, slope_ref, space_sum_ref, moved_ref, out_hbm, sum_ref, out_ref, out_sem
):
    frames = moved_ref.shape[0]
    heads = moved_ref.shape[1]
    rows = moved_ref.shape[2] // 4
    size = frames * STEP
    steps = rows // STEP
    group = lax.rem(lax.axis_index("seq"), HEAD_SPLIT)
    frame_count = fc_ref[lax.axis_index("dp")]
    row = lax.broadcasted_iota(jnp.int32, (size, size), 0)
    col = lax.broadcasted_iota(jnp.int32, (size, size), 1)
    row_frame, col_frame = row // STEP, col // STEP
    distance = jnp.abs(row_frame - col_frame).astype(jnp.float32)
    live = (lax.rem(row, STEP) == lax.rem(col, STEP)) & (row_frame < frame_count)
    sums = space_sum_ref[...]
    lane = lax.broadcasted_iota(jnp.int32, sums.shape, 1)
    sending = []
    for head in range(heads):
        which = group * heads + head
        factor = scale_ref[which] * (1.0 / math.sqrt(HEAD))
        bias = jnp.where(live, -slope_ref[which] * distance, -jnp.inf)

        def load(index, step):
            part = moved_ref[:, head, pl.ds(index * rows + step * STEP, STEP), :]
            return part.astype(jnp.float32).reshape(size, HEAD).astype(jnp.bfloat16)

        def store(index, step, value):
            value = value.reshape(frames, STEP, HEAD).astype(jnp.bfloat16)
            out_ref[:, head, pl.ds(index * rows + step * STEP, STEP), :] = value

        scale_terms = jnp.zeros((size, size), jnp.float32)
        slope_terms = jnp.zeros((size, size), jnp.float32)
        for first in range(0, steps, BATCH):
            batch = range(first, min(first + BATCH, steps))
            parts = [[load(index, step) for index in range(4)] for step in batch]
            raws = [dot(key, query, AB_T) for query, key, _, _ in parts]
            grad_probs = [dot(value, grad, AB_T) for _, _, value, grad in parts]
            scores = [raw * factor + bias for raw in raws]
            exponents = [jnp.exp(x - jnp.max(x, axis=0, keepdims=True)) for x in scores]
            probs = [x * (1.0 / jnp.sum(x, axis=0, keepdims=True)) for x in exponents]
            weighted = [x * y for x, y in zip(probs, grad_probs)]
            grad_scores = [
                x - y * jnp.sum(x, axis=0, keepdims=True) for x, y in zip(weighted, probs)
            ]
            for x, raw in zip(grad_scores, raws):
                scale_terms += x * raw
                slope_terms += x
            for step, (query, key, _, grad), prob, x in zip(batch, parts, probs, grad_scores):
                rounded = x.astype(jnp.bfloat16)
                store(0, step, dot(rounded, key, A_TB) * factor)
                store(1, step, dot(rounded, query, AB) * factor)
                store(2, step, dot(prob.astype(jnp.bfloat16), grad, AB))
        sent = pltpu.make_async_copy(
            out_ref.at[:, head], out_hbm.at[:, head], out_sem.at[head]
        )
        sent.start()
        sending.append(sent)
        scale_sum = jnp.sum(scale_terms) * (1.0 / math.sqrt(HEAD))
        slope_sum = -jnp.sum(slope_terms * distance)
        sums = sums + jnp.where(lane == which, scale_sum, 0.0)
        sums = sums + jnp.where(lane == heads * HEAD_SPLIT + which, slope_sum, 0.0)
    sum_ref[...] = jnp.broadcast_to(sums[None], sum_ref.shape)
    for sent in sending:
        sent.wait()


def time(frame_counts, head_scale, frame_slope, space_sum, moved):
    frames, heads, height, _ = moved.shape
    rows = height // 4
    smem = pl.BlockSpec(memory_space=pltpu.SMEM)
    vmem = pl.BlockSpec(memory_space=pltpu.VMEM)
    return pl.pallas_call(
        time_kernel,
        in_specs=[smem] * 3 + [vmem] * 2,
        out_specs=[pl.BlockSpec(memory_space=pltpu.HBM), vmem],
        out_shape=[
            pltpu.HBM((frames, heads, 3 * rows, HEAD), jnp.bfloat16),
            jax.ShapeDtypeStruct((frames, 1, HEAD), jnp.float32),
        ],
        scratch_shapes=[
            pltpu.VMEM((frames, heads, 3 * rows, HEAD), jnp.bfloat16),
            pltpu.SemaphoreType.DMA((heads,)),
        ],
        compiler_params=pltpu.CompilerParams(vmem_limit_bytes=SCOPED),
        cost_estimate=pl.CostEstimate(
            flops=10 * heads * rows * frames * frames * STEP * HEAD,
            bytes_accessed=14 * frames * rows * heads * HEAD,
            transcendentals=heads * rows * frames * frames * STEP,
        ),
        name="time",
    )(frame_counts, head_scale, frame_slope, space_sum, moved)


def add_kernel(back_ref, q_ref, k_ref, v_ref, oq_ref, ok_ref, ov_ref):
    rows = q_ref.shape[0] // ROW_SPLIT
    for index, (ref, out) in enumerate(((q_ref, oq_ref), (k_ref, ok_ref), (v_ref, ov_ref))):
        for part in range(ROW_SPLIT):
            for head in range(back_ref.shape[2]):
                here = (pl.ds(part * rows, rows), pl.ds(head * HEAD, HEAD))
                moved = back_ref[part, 0, head, pl.ds(index * rows, rows), :].astype(jnp.float32)
                out[here] = (ref[here] + moved).astype(jnp.bfloat16)


def add(back, arrays):
    spatial, channels = arrays[0].shape
    width = channels // HEAD_SPLIT
    rows = spatial // ROW_SPLIT
    block = pl.BlockSpec((spatial, width), lambda i: (0, i))
    return pl.pallas_call(
        add_kernel,
        grid=(HEAD_SPLIT,),
        in_specs=[
            pl.BlockSpec((ROW_SPLIT, 1, width // HEAD, 3 * rows, HEAD), lambda i: (0, i, 0, 0, 0))
        ]
        + [block] * 3,
        out_specs=[block] * 3,
        out_shape=[jax.ShapeDtypeStruct((spatial, channels), jnp.bfloat16)] * 3,
        compiler_params=pltpu.CompilerParams(vmem_limit_bytes=SCOPED),
        cost_estimate=pl.CostEstimate(
            flops=3 * spatial * channels, bytes_accessed=24 * spatial * channels, transcendentals=0
        ),
        name="add",
    )(back, *arrays)


def local(
    queries, key_rows, values, cotangent, frame_counts, position_counts, head_scale, frame_slope
):
    spatial, channels = queries.shape[2:]
    heads = head_scale.shape[0]
    clips = lax.axis_size("dp")
    arrays = [x.reshape(spatial, channels) for x in (queries, key_rows, values, cotangent)]
    exchange = functools.partial(
        lax.all_to_all, axis_name="seq", split_axis=0, concat_axis=0, tiled=True
    )
    packed = pack(frame_counts, position_counts, arrays)
    moved = exchange(packed)
    *space_grads, space_sum = space(frame_counts, position_counts, head_scale, arrays)
    grads, sums = time(frame_counts, head_scale, frame_slope, space_sum, moved)
    back = exchange(grads)
    stride = 1
    while stride < clips:
        sums = sums + lax.ppermute(sums, "dp", [(i, i ^ stride) for i in range(clips)])
        stride *= 2
    sums, back = lax.optimization_barrier((sums, back))
    sums = jnp.sum(exchange(sums), axis=(0, 1))
    back = back.reshape((ROW_SPLIT, HEAD_SPLIT) + back.shape[1:])
    outputs = add(back, space_grads)
    full = queries.shape
    return tuple(x.reshape(full) for x in outputs) + (sums[:heads], sums[heads : 2 * heads])


def solution(mesh):
    split = P("dp", "seq", None, None)
    return jax.shard_map(
        local,
        mesh=mesh,
        in_specs=(split,) * 4 + (P(),) * 4,
        out_specs=(split,) * 3 + (P(),) * 2,
        check_vma=False,
    )
```

```python
import functools
import math

import jax
import jax.numpy as jnp
from jax import lax
from jax.experimental import pallas as pl
from jax.experimental.pallas import tpu as pltpu
from jax.sharding import PartitionSpec as P

HEAD = 128
ROW_SPLIT = 4
HEAD_SPLIT = 4
STEP = 8
BATCH = 7
SPACE_TYPE = jnp.float32
SCOPED = 32 * 2**20
STREAM = 60 * 2**20


def dot(a, b, dims):
    return lax.dot_general(a, b, (dims, ((), ())), preferred_element_type=jnp.float32)


DISTANCES = {4: ((2, 1), (0, -1)), 8: ((4, -3), (3, -2), (0, 2), (1, -1))}

AB_T = ((1,), (1,))
AB = ((1,), (0,))
A_TB = ((0,), (0,))


def live_rows(fc_ref, pc_ref, shape):
    clip = lax.axis_index("dp")
    positions = jnp.where(lax.axis_index("seq") < fc_ref[clip], pc_ref[clip], 0)
    return lax.broadcasted_iota(jnp.int32, shape, 0) < positions


def pack_kernel(
    fc_hbm,
    pc_hbm,
    q_hbm,
    k_hbm,
    v_hbm,
    g_hbm,
    out_hbm,
    fc_ref,
    pc_ref,
    held_ref,
    out_ref,
    count_sem,
    in_sem,
    out_sem,
):
    spatial = held_ref.shape[1]
    rows = spatial // ROW_SPLIT
    heads = out_ref.shape[1]
    width = heads * HEAD

    def fetch(index, group):
        here = pl.ds(group * width, width)
        return pltpu.make_async_copy(
            (q_hbm, k_hbm, v_hbm, g_hbm)[index].at[:, here],
            held_ref.at[index, :, here],
            in_sem.at[group, index],
        )

    def send(group):
        here = pl.ds(group * ROW_SPLIT, ROW_SPLIT)
        return pltpu.make_async_copy(out_ref.at[here], out_hbm.at[here], out_sem.at[group])

    counts = (
        pltpu.make_async_copy(fc_hbm, fc_ref, count_sem.at[0]),
        pltpu.make_async_copy(pc_hbm, pc_ref, count_sem.at[1]),
    )
    for index in range(4):
        fetch(index, 0).start()
    for count in counts:
        count.start()
    for group in range(1, HEAD_SPLIT):
        for index in range(4):
            fetch(index, group).start()
    for group in range(HEAD_SPLIT):
        for index in range(4):
            fetch(index, group).wait()
            if group == 0 and index == 3:
                for count in counts:
                    count.wait()
                live = live_rows(fc_ref, pc_ref, (spatial, width))
            value = held_ref[index, :, pl.ds(group * width, width)]
            if index == 3:
                value = jnp.where(live, value, 0).astype(jnp.bfloat16)
            for part in range(ROW_SPLIT):
                for head in range(heads):
                    out_ref[group * ROW_SPLIT + part, head, pl.ds(index * rows, rows), :] = value[
                        part * rows : (part + 1) * rows, head * HEAD : (head + 1) * HEAD
                    ]
        send(group).start()
    for group in range(HEAD_SPLIT):
        send(group).wait()


def pack(frame_counts, position_counts, arrays):
    spatial, channels = arrays[0].shape
    rows = spatial // ROW_SPLIT
    hbm = pl.BlockSpec(memory_space=pltpu.HBM)
    shape = (ROW_SPLIT * HEAD_SPLIT, channels // (HEAD * HEAD_SPLIT), 4 * rows, HEAD)
    return pl.pallas_call(
        pack_kernel,
        in_specs=[hbm] * 6,
        out_specs=hbm,
        out_shape=pltpu.HBM(shape, jnp.bfloat16),
        scratch_shapes=[
            pltpu.SMEM(frame_counts.shape, jnp.int32),
            pltpu.SMEM(position_counts.shape, jnp.int32),
            pltpu.VMEM((4, spatial, channels), jnp.bfloat16),
            pltpu.VMEM(shape, jnp.bfloat16),
            pltpu.SemaphoreType.DMA((2,)),
            pltpu.SemaphoreType.DMA((HEAD_SPLIT, 4)),
            pltpu.SemaphoreType.DMA((HEAD_SPLIT,)),
        ],
        compiler_params=pltpu.CompilerParams(vmem_limit_bytes=STREAM),
        cost_estimate=pl.CostEstimate(
            flops=0, bytes_accessed=4 * 4 * spatial * channels, transcendentals=0
        ),
        name="pack",
    )(frame_counts, position_counts, *arrays)


def space_kernel(
    fc_ref, pc_ref, scale_ref, q_ref, k_ref, v_ref, g_ref, dq_ref, dk_ref, dv_ref, sum_ref
):
    head = pl.program_id(0)
    factor = scale_ref[head] * (1.0 / math.sqrt(HEAD))
    query, key, value = q_ref[...], k_ref[...], v_ref[...]
    grad = g_ref[...]
    grad = jnp.where(live_rows(fc_ref, pc_ref, grad.shape), grad, 0).astype(grad.dtype)
    raw = dot(key, query, AB_T)
    key_row = lax.broadcasted_iota(jnp.int32, raw.shape, 0)
    live = key_row < pc_ref[lax.axis_index("dp")]
    scores = jnp.where(live, raw * factor, -jnp.inf)
    exponent = jnp.exp(scores - jnp.max(scores, axis=0, keepdims=True))
    prob = exponent * (1.0 / jnp.sum(exponent, axis=0, keepdims=True))
    grad_prob = dot(value, grad, AB_T)
    weighted = prob * grad_prob
    grad_score = weighted - prob * jnp.sum(weighted, axis=0, keepdims=True)
    rounded = grad_score.astype(jnp.bfloat16)
    dq_ref[...] = (dot(rounded, key, A_TB) * factor).astype(dq_ref.dtype)
    dk_ref[...] = (dot(rounded, query, AB) * factor).astype(dk_ref.dtype)
    dv_ref[...] = dot(prob.astype(jnp.bfloat16), grad, AB).astype(dv_ref.dtype)
    term = jnp.sum(grad_score * raw) * (1.0 / math.sqrt(HEAD))
    lane = lax.broadcasted_iota(jnp.int32, sum_ref.shape, 1)

    @pl.when(head == 0)
    def _():
        sum_ref[...] = jnp.zeros_like(sum_ref)

    sum_ref[...] += jnp.where(lane == head, term, 0.0)


def space(frame_counts, position_counts, head_scale, arrays):
    spatial, channels = arrays[0].shape
    heads = channels // HEAD
    smem = pl.BlockSpec(memory_space=pltpu.SMEM)
    block = pl.BlockSpec((spatial, HEAD), lambda i: (0, i))
    return pl.pallas_call(
        space_kernel,
        grid=(heads,),
        in_specs=[smem] * 3 + [block] * 4,
        out_specs=[block] * 3 + [pl.BlockSpec((1, HEAD), lambda i: (0, 0))],
        out_shape=[jax.ShapeDtypeStruct((spatial, channels), SPACE_TYPE)] * 3
        + [jax.ShapeDtypeStruct((1, HEAD), jnp.float32)],
        compiler_params=pltpu.CompilerParams(vmem_limit_bytes=SCOPED),
        cost_estimate=pl.CostEstimate(
            flops=10 * heads * spatial * spatial * HEAD,
            bytes_accessed=20 * spatial * channels,
            transcendentals=heads * spatial * spatial,
        ),
        name="space",
    )(frame_counts, position_counts, head_scale, *arrays)


def time_kernel(
    fc_ref, scale_ref, slope_ref, space_sum_ref, moved_ref, out_hbm, sum_ref, out_ref, out_sem
):
    frames = moved_ref.shape[0]
    heads = moved_ref.shape[1]
    rows = moved_ref.shape[2] // 4
    size = frames * STEP
    steps = rows // STEP
    group = lax.div(lax.axis_index("seq"), ROW_SPLIT)
    frame_count = fc_ref[lax.axis_index("dp")]
    row = lax.broadcasted_iota(jnp.int32, (size, size), 0)
    col = lax.broadcasted_iota(jnp.int32, (size, size), 1)
    row_frame, col_frame = row // STEP, col // STEP
    distance = jnp.abs(row_frame - col_frame).astype(jnp.float32)
    live = (lax.rem(row, STEP) == lax.rem(col, STEP)) & (row_frame < frame_count)
    sums = space_sum_ref[...]
    lane = lax.broadcasted_iota(jnp.int32, sums.shape, 1)
    sending = []
    for head in range(heads):
        which = group * heads + head
        factor = scale_ref[which] * (1.0 / math.sqrt(HEAD))
        bias = jnp.where(live, -slope_ref[which] * distance, -jnp.inf)

        def load(index, step):
            part = moved_ref[:, head, pl.ds(index * rows + step * STEP, STEP), :]
            return part.astype(jnp.float32).reshape(size, HEAD).astype(jnp.bfloat16)

        def store(index, step, value):
            value = value.reshape(frames, STEP, HEAD).astype(jnp.bfloat16)
            out_ref[:, head, pl.ds(index * rows + step * STEP, STEP), :] = value

        scale_terms = jnp.zeros((size, size), jnp.float32)
        slope_terms = jnp.zeros((size, size), jnp.float32)
        for first in range(0, steps, BATCH):
            batch = range(first, min(first + BATCH, steps))
            parts = [[load(index, step) for index in range(4)] for step in batch]
            raws = [dot(key, query, AB_T) for query, key, _, _ in parts]
            grad_probs = [dot(value, grad, AB_T) for _, _, value, grad in parts]
            scores = [raw * factor + bias for raw in raws]
            exponents = [jnp.exp(x - jnp.max(x, axis=0, keepdims=True)) for x in scores]
            probs = [x * (1.0 / jnp.sum(x, axis=0, keepdims=True)) for x in exponents]
            weighted = [x * y for x, y in zip(probs, grad_probs)]
            grad_scores = [
                x - y * jnp.sum(x, axis=0, keepdims=True) for x, y in zip(weighted, probs)
            ]
            for x, raw in zip(grad_scores, raws):
                scale_terms += x * raw
                slope_terms += x
            for step, (query, key, _, grad), prob, x in zip(batch, parts, probs, grad_scores):
                rounded = x.astype(jnp.bfloat16)
                store(0, step, dot(rounded, key, A_TB) * factor)
                store(1, step, dot(rounded, query, AB) * factor)
                store(2, step, dot(prob.astype(jnp.bfloat16), grad, AB))
        sent = pltpu.make_async_copy(
            out_ref.at[:, head], out_hbm.at[:, head], out_sem.at[head]
        )
        sent.start()
        sending.append(sent)
        scale_sum = jnp.sum(scale_terms) * (1.0 / math.sqrt(HEAD))
        slope_sum = -jnp.sum(slope_terms * distance)
        sums = sums + jnp.where(lane == which, scale_sum, 0.0)
        sums = sums + jnp.where(lane == heads * HEAD_SPLIT + which, slope_sum, 0.0)
    sum_ref[...] = sums
    for sent in sending:
        sent.wait()


def time(frame_counts, head_scale, frame_slope, space_sum, moved):
    frames, heads, height, _ = moved.shape
    rows = height // 4
    smem = pl.BlockSpec(memory_space=pltpu.SMEM)
    vmem = pl.BlockSpec(memory_space=pltpu.VMEM)
    return pl.pallas_call(
        time_kernel,
        in_specs=[smem] * 3 + [vmem] * 2,
        out_specs=[pl.BlockSpec(memory_space=pltpu.HBM), vmem],
        out_shape=[
            pltpu.HBM((frames, heads, 3 * rows, HEAD), jnp.bfloat16),
            jax.ShapeDtypeStruct((1, HEAD), jnp.float32),
        ],
        scratch_shapes=[
            pltpu.VMEM((frames, heads, 3 * rows, HEAD), jnp.bfloat16),
            pltpu.SemaphoreType.DMA((heads,)),
        ],
        compiler_params=pltpu.CompilerParams(vmem_limit_bytes=SCOPED),
        cost_estimate=pl.CostEstimate(
            flops=10 * heads * rows * frames * frames * STEP * HEAD,
            bytes_accessed=14 * frames * rows * heads * HEAD,
            transcendentals=heads * rows * frames * frames * STEP,
        ),
        name="time",
    )(frame_counts, head_scale, frame_slope, space_sum, moved)


def add_kernel(
    back_ref, q_hbm, k_hbm, v_hbm, oq_hbm, ok_hbm, ov_hbm, held_ref, out_ref, in_sem, out_sem
):
    rows = held_ref.shape[1] // ROW_SPLIT
    heads = back_ref.shape[2]
    width = heads * HEAD

    def fetch(index, group):
        here = pl.ds(group * width, width)
        return pltpu.make_async_copy(
            (q_hbm, k_hbm, v_hbm)[index].at[:, here],
            held_ref.at[index, :, here],
            in_sem.at[group, index],
        )

    def send(index, group):
        here = pl.ds(group * width, width)
        return pltpu.make_async_copy(
            out_ref.at[index, :, here],
            (oq_hbm, ok_hbm, ov_hbm)[index].at[:, here],
            out_sem.at[group, index],
        )

    blocks = [(index, group) for group in range(HEAD_SPLIT) for index in range(3)]
    for block in blocks:
        fetch(*block).start()
    for index, group in blocks:
        fetch(index, group).wait()
        for head in range(heads):
            columns = pl.ds(group * width + head * HEAD, HEAD)
            moved = [
                back_ref[group, part, head, pl.ds(index * rows, rows), :].astype(jnp.float32)
                for part in range(ROW_SPLIT)
            ]
            total = held_ref[index, :, columns].astype(jnp.float32) + jnp.concatenate(moved, axis=0)
            out_ref[index, :, columns] = total.astype(jnp.bfloat16)
        send(index, group).start()
    for block in blocks:
        send(*block).wait()


def add(back, arrays):
    spatial, channels = arrays[0].shape
    hbm = pl.BlockSpec(memory_space=pltpu.HBM)
    return pl.pallas_call(
        add_kernel,
        in_specs=[pl.BlockSpec(memory_space=pltpu.VMEM)] + [hbm] * 3,
        out_specs=[hbm] * 3,
        out_shape=[pltpu.HBM((spatial, channels), jnp.bfloat16)] * 3,
        scratch_shapes=[
            pltpu.VMEM((3, spatial, channels), arrays[0].dtype),
            pltpu.VMEM((3, spatial, channels), jnp.bfloat16),
            pltpu.SemaphoreType.DMA((HEAD_SPLIT, 3)),
            pltpu.SemaphoreType.DMA((HEAD_SPLIT, 3)),
        ],
        compiler_params=pltpu.CompilerParams(vmem_limit_bytes=SCOPED),
        cost_estimate=pl.CostEstimate(
            flops=3 * spatial * channels, bytes_accessed=24 * spatial * channels, transcendentals=0
        ),
        name="add",
    )(back, *[pltpu.with_memory_space_constraint(x, pltpu.HBM) for x in arrays])


def core_sum(sums):
    cores = [[2 * i, 2 * i + 1] for i in range(lax.axis_size("seq") // 2)]
    both = lax.all_gather(sums, "seq", axis=0, tiled=True, axis_index_groups=cores)
    return jnp.sum(both, axis=0, keepdims=True)


def ring_parts(sums, axis, stride, size):
    clips, places = lax.axis_size("dp"), lax.axis_size("seq")
    own = jnp.where(lax.rem(lax.axis_index("seq"), 2) == 0, sums, 0.0)
    if size > lax.axis_size(axis) // stride:
        return [own]

    def source(clip, place, distance):
        index = place if axis == "seq" else clip
        here = index // stride % size
        index += ((here + distance) % size - here) * stride
        return (clip, index) if axis == "seq" else (index, place)

    def receive(first, second):
        pairs = []
        for clip in range(clips):
            for place in range(places):
                distance = (first, second)[place % 2]
                if distance:
                    from_clip, from_place = source(clip, place, distance)
                    pairs.append((from_clip * places + from_place, clip * places + place))
        return lax.ppermute(sums, ("dp", "seq"), pairs)

    return [own] + [receive(first, second) for first, second in DISTANCES[size]]


def local(
    queries, key_rows, values, cotangent, frame_counts, position_counts, head_scale, frame_slope
):
    spatial, channels = queries.shape[2:]
    heads = head_scale.shape[0]
    arrays = [x.reshape(spatial, channels) for x in (queries, key_rows, values, cotangent)]
    exchange = functools.partial(
        lax.all_to_all, axis_name="seq", split_axis=0, concat_axis=0, tiled=True
    )
    packed = pack(frame_counts, position_counts, arrays)
    moved = exchange(packed)
    *space_grads, space_sum = space(frame_counts, position_counts, head_scale, arrays)
    grads, sums = time(frame_counts, head_scale, frame_slope, space_sum, moved)
    back = exchange(grads)
    sums = core_sum(sums)
    sums = core_sum(sum(ring_parts(sums, "dp", 1, 4)))
    clips = lax.axis_size("dp")
    for stride in (4, 8, 16):
        if stride < clips:
            sums = sums + lax.ppermute(sums, "dp", [(i, i ^ stride) for i in range(clips)])
    parts = ring_parts(sums, "seq", 2, 8)
    back = back.reshape((HEAD_SPLIT, ROW_SPLIT) + back.shape[1:])
    outputs = add(back, space_grads)
    outputs, parts = lax.optimization_barrier((outputs, parts))
    sums = core_sum(sum(parts))[0]
    full = queries.shape
    return tuple(x.reshape(full) for x in outputs) + (sums[:heads], sums[heads : 2 * heads])


def solution(mesh):
    split = P("dp", "seq", None, None)
    return jax.shard_map(
        local,
        mesh=mesh,
        in_specs=(split,) * 4 + (P(),) * 4,
        out_specs=(split,) * 3 + (P(),) * 2,
        check_vma=False,
    )
```

```python
import functools
import math

import jax
import jax.numpy as jnp
from jax import lax
from jax.experimental import pallas as pl
from jax.experimental.pallas import tpu as pltpu
from jax.sharding import PartitionSpec as P

HEAD = 128
ROW_SPLIT = 4
HEAD_SPLIT = 4
STEP = 8
BATCH = 7
SPACE_TYPE = jnp.bfloat16
SCOPED = 32 * 2**20
STREAM = 60 * 2**20


def dot(a, b, dims):
    return lax.dot_general(a, b, (dims, ((), ())), preferred_element_type=jnp.float32)


DISTANCES = {4: ((2, 1), (0, -1)), 8: ((4, -3), (3, -2), (0, 2), (1, -1))}

AB_T = ((1,), (1,))
AB = ((1,), (0,))
A_TB = ((0,), (0,))


def live_rows(fc_ref, pc_ref, shape):
    clip = lax.axis_index("dp")
    positions = jnp.where(lax.axis_index("seq") < fc_ref[clip], pc_ref[clip], 0)
    return lax.broadcasted_iota(jnp.int32, shape, 0) < positions


def pack_kernel(
    fc_hbm,
    pc_hbm,
    q_hbm,
    k_hbm,
    v_hbm,
    g_hbm,
    out_hbm,
    fc_ref,
    pc_ref,
    held_ref,
    out_ref,
    count_sem,
    in_sem,
    out_sem,
):
    spatial = held_ref.shape[1]
    rows = spatial // ROW_SPLIT
    heads = out_ref.shape[1]
    width = heads * HEAD

    def fetch(index, group):
        here = pl.ds(group * width, width)
        return pltpu.make_async_copy(
            (q_hbm, k_hbm, v_hbm, g_hbm)[index].at[:, here],
            held_ref.at[index, :, here],
            in_sem.at[group, index],
        )

    def send(group):
        here = pl.ds(group * ROW_SPLIT, ROW_SPLIT)
        return pltpu.make_async_copy(out_ref.at[here], out_hbm.at[here], out_sem.at[group])

    counts = (
        pltpu.make_async_copy(fc_hbm, fc_ref, count_sem.at[0]),
        pltpu.make_async_copy(pc_hbm, pc_ref, count_sem.at[1]),
    )
    for index in range(4):
        fetch(index, 0).start()
    for count in counts:
        count.start()
    for group in range(1, HEAD_SPLIT):
        for index in range(4):
            fetch(index, group).start()
    for group in range(HEAD_SPLIT):
        for index in range(4):
            fetch(index, group).wait()
            if group == 0 and index == 3:
                for count in counts:
                    count.wait()
                live = live_rows(fc_ref, pc_ref, (spatial, width))
            value = held_ref[index, :, pl.ds(group * width, width)]
            if index == 3:
                value = jnp.where(live, value, 0).astype(jnp.bfloat16)
            for part in range(ROW_SPLIT):
                for head in range(heads):
                    out_ref[group * ROW_SPLIT + part, head, pl.ds(index * rows, rows), :] = value[
                        part * rows : (part + 1) * rows, head * HEAD : (head + 1) * HEAD
                    ]
        send(group).start()
    for group in range(HEAD_SPLIT):
        send(group).wait()


def pack(frame_counts, position_counts, arrays):
    spatial, channels = arrays[0].shape
    rows = spatial // ROW_SPLIT
    hbm = pl.BlockSpec(memory_space=pltpu.HBM)
    shape = (ROW_SPLIT * HEAD_SPLIT, channels // (HEAD * HEAD_SPLIT), 4 * rows, HEAD)
    return pl.pallas_call(
        pack_kernel,
        in_specs=[hbm] * 6,
        out_specs=hbm,
        out_shape=pltpu.HBM(shape, jnp.bfloat16),
        scratch_shapes=[
            pltpu.SMEM(frame_counts.shape, jnp.int32),
            pltpu.SMEM(position_counts.shape, jnp.int32),
            pltpu.VMEM((4, spatial, channels), jnp.bfloat16),
            pltpu.VMEM(shape, jnp.bfloat16),
            pltpu.SemaphoreType.DMA((2,)),
            pltpu.SemaphoreType.DMA((HEAD_SPLIT, 4)),
            pltpu.SemaphoreType.DMA((HEAD_SPLIT,)),
        ],
        compiler_params=pltpu.CompilerParams(vmem_limit_bytes=STREAM),
        cost_estimate=pl.CostEstimate(
            flops=0, bytes_accessed=4 * 4 * spatial * channels, transcendentals=0
        ),
        name="pack",
    )(frame_counts, position_counts, *arrays)


def space_kernel(
    fc_ref, pc_ref, scale_ref, q_ref, k_ref, v_ref, g_ref, dq_ref, dk_ref, dv_ref, sum_ref
):
    head = pl.program_id(0)
    factor = scale_ref[head] * (1.0 / math.sqrt(HEAD))
    query, key, value = q_ref[...], k_ref[...], v_ref[...]
    grad = g_ref[...]
    grad = jnp.where(live_rows(fc_ref, pc_ref, grad.shape), grad, 0).astype(grad.dtype)
    raw = dot(key, query, AB_T)
    key_row = lax.broadcasted_iota(jnp.int32, raw.shape, 0)
    live = key_row < pc_ref[lax.axis_index("dp")]
    scores = jnp.where(live, raw * factor, -jnp.inf)
    exponent = jnp.exp(scores - jnp.max(scores, axis=0, keepdims=True))
    prob = exponent * (1.0 / jnp.sum(exponent, axis=0, keepdims=True))
    grad_prob = dot(value, grad, AB_T)
    weighted = prob * grad_prob
    grad_score = weighted - prob * jnp.sum(weighted, axis=0, keepdims=True)
    rounded = grad_score.astype(jnp.bfloat16)
    here = pl.ds(head * HEAD, HEAD)
    dq_ref[:, here] = (dot(rounded, key, A_TB) * factor).astype(dq_ref.dtype)
    dk_ref[:, here] = (dot(rounded, query, AB) * factor).astype(dk_ref.dtype)
    dv_ref[:, here] = dot(prob.astype(jnp.bfloat16), grad, AB).astype(dv_ref.dtype)
    term = jnp.sum(grad_score * raw) * (1.0 / math.sqrt(HEAD))
    lane = lax.broadcasted_iota(jnp.int32, sum_ref.shape, 1)

    @pl.when(head == 0)
    def _():
        sum_ref[...] = jnp.zeros_like(sum_ref)

    sum_ref[...] += jnp.where(lane == head, term, 0.0)


def space(frame_counts, position_counts, head_scale, arrays):
    spatial, channels = arrays[0].shape
    heads = channels // HEAD
    smem = pl.BlockSpec(memory_space=pltpu.SMEM)
    vmem = pl.BlockSpec(memory_space=pltpu.VMEM)
    block = pl.BlockSpec((spatial, HEAD), lambda i: (0, i))
    return pl.pallas_call(
        space_kernel,
        grid=(heads,),
        in_specs=[smem] * 3 + [block] * 4,
        out_specs=[vmem] * 3 + [pl.BlockSpec((1, HEAD), lambda i: (0, 0))],
        out_shape=[pltpu.VMEM((spatial, channels), SPACE_TYPE)] * 3
        + [jax.ShapeDtypeStruct((1, HEAD), jnp.float32)],
        compiler_params=pltpu.CompilerParams(vmem_limit_bytes=SCOPED),
        cost_estimate=pl.CostEstimate(
            flops=10 * heads * spatial * spatial * HEAD,
            bytes_accessed=20 * spatial * channels,
            transcendentals=heads * spatial * spatial,
        ),
        name="space",
    )(frame_counts, position_counts, head_scale, *arrays)


def time_kernel(
    fc_hbm,
    scale_hbm,
    slope_hbm,
    space_sum_hbm,
    moved_ref,
    out_hbm,
    sum_ref,
    fc_ref,
    scale_ref,
    slope_ref,
    space_sum_ref,
    out_ref,
    small_sem,
    out_sem,
):
    smalls = [
        pltpu.make_async_copy(source, target, small_sem.at[index])
        for index, (source, target) in enumerate(
            (
                (fc_hbm, fc_ref),
                (scale_hbm, scale_ref),
                (slope_hbm, slope_ref),
                (space_sum_hbm, space_sum_ref),
            )
        )
    ]
    for small in smalls:
        small.start()
    frames = moved_ref.shape[0]
    heads = moved_ref.shape[1]
    rows = moved_ref.shape[2] // 4
    size = frames * STEP
    steps = rows // STEP
    group = lax.div(lax.axis_index("seq"), ROW_SPLIT)
    row = lax.broadcasted_iota(jnp.int32, (size, size), 0)
    col = lax.broadcasted_iota(jnp.int32, (size, size), 1)
    row_frame, col_frame = row // STEP, col // STEP
    distance = jnp.abs(row_frame - col_frame).astype(jnp.float32)
    same = lax.rem(row, STEP) == lax.rem(col, STEP)
    sums = jnp.zeros(sum_ref.shape, jnp.float32)
    lane = lax.broadcasted_iota(jnp.int32, sums.shape, 1)
    sending = []
    for head in range(heads):
        which = group * heads + head

        def load(index, step):
            part = moved_ref[:, head, pl.ds(index * rows + step * STEP, STEP), :]
            return part.astype(jnp.float32).reshape(size, HEAD).astype(jnp.bfloat16)

        def store(index, step, value):
            value = value.reshape(frames, STEP, HEAD).astype(jnp.bfloat16)
            out_ref[:, head, pl.ds(index * rows + step * STEP, STEP), :] = value

        scale_terms = jnp.zeros((size, size), jnp.float32)
        slope_terms = jnp.zeros((size, size), jnp.float32)
        for first in range(0, steps, BATCH):
            batch = range(first, min(first + BATCH, steps))
            parts = [[load(index, step) for index in range(4)] for step in batch]
            raws = [dot(key, query, AB_T) for query, key, _, _ in parts]
            grad_probs = [dot(value, grad, AB_T) for _, _, value, grad in parts]
            if first == 0:
                if head == 0:
                    for small in smalls:
                        small.wait()
                    live = same & (row_frame < fc_ref[lax.axis_index("dp")])
                    sums = space_sum_ref[...]
                factor = scale_ref[which] * (1.0 / math.sqrt(HEAD))
                bias = jnp.where(live, -slope_ref[which] * distance, -jnp.inf)
            scores = [raw * factor + bias for raw in raws]
            exponents = [jnp.exp(x - jnp.max(x, axis=0, keepdims=True)) for x in scores]
            probs = [x * (1.0 / jnp.sum(x, axis=0, keepdims=True)) for x in exponents]
            weighted = [x * y for x, y in zip(probs, grad_probs)]
            grad_scores = [
                x - y * jnp.sum(x, axis=0, keepdims=True) for x, y in zip(weighted, probs)
            ]
            for x, raw in zip(grad_scores, raws):
                scale_terms += x * raw
                slope_terms += x
            for step, (query, key, _, grad), prob, x in zip(batch, parts, probs, grad_scores):
                rounded = x.astype(jnp.bfloat16)
                store(0, step, dot(rounded, key, A_TB) * factor)
                store(1, step, dot(rounded, query, AB) * factor)
                store(2, step, dot(prob.astype(jnp.bfloat16), grad, AB))
        sent = pltpu.make_async_copy(
            out_ref.at[:, head], out_hbm.at[:, head], out_sem.at[head]
        )
        sent.start()
        sending.append(sent)
        scale_sum = jnp.sum(scale_terms) * (1.0 / math.sqrt(HEAD))
        slope_sum = -jnp.sum(slope_terms * distance)
        sums = sums + jnp.where(lane == which, scale_sum, 0.0)
        sums = sums + jnp.where(lane == heads * HEAD_SPLIT + which, slope_sum, 0.0)
    sum_ref[...] = sums
    for sent in sending:
        sent.wait()


def time(frame_counts, head_scale, frame_slope, space_sum, moved):
    frames, heads, height, _ = moved.shape
    rows = height // 4
    hbm = pl.BlockSpec(memory_space=pltpu.HBM)
    vmem = pl.BlockSpec(memory_space=pltpu.VMEM)
    return pl.pallas_call(
        time_kernel,
        in_specs=[hbm] * 4 + [vmem],
        out_specs=[hbm, vmem],
        out_shape=[
            pltpu.HBM((frames, heads, 3 * rows, HEAD), jnp.bfloat16),
            jax.ShapeDtypeStruct((1, HEAD), jnp.float32),
        ],
        scratch_shapes=[
            pltpu.SMEM(frame_counts.shape, jnp.int32),
            pltpu.SMEM(head_scale.shape, jnp.float32),
            pltpu.SMEM(frame_slope.shape, jnp.float32),
            pltpu.VMEM(space_sum.shape, jnp.float32),
            pltpu.VMEM((frames, heads, 3 * rows, HEAD), jnp.bfloat16),
            pltpu.SemaphoreType.DMA((4,)),
            pltpu.SemaphoreType.DMA((heads,)),
        ],
        compiler_params=pltpu.CompilerParams(vmem_limit_bytes=SCOPED),
        cost_estimate=pl.CostEstimate(
            flops=10 * heads * rows * frames * frames * STEP * HEAD,
            bytes_accessed=14 * frames * rows * heads * HEAD,
            transcendentals=heads * rows * frames * frames * STEP,
        ),
        name="time",
    )(frame_counts, head_scale, frame_slope, space_sum, moved)


def add_kernel(
    back_ref, dq_ref, dk_ref, dv_ref, oq_hbm, ok_hbm, ov_hbm, out_ref, out_sem
):
    rows = dv_ref.shape[0] // ROW_SPLIT
    heads = back_ref.shape[2]
    width = heads * HEAD

    def send(index, group):
        here = pl.ds(group * width, width)
        return pltpu.make_async_copy(
            out_ref.at[index, :, here],
            (oq_hbm, ok_hbm, ov_hbm)[index].at[:, here],
            out_sem.at[group, index],
        )

    blocks = [(index, group) for index in range(3) for group in range(HEAD_SPLIT)]
    for index, group in blocks:
        for head in range(heads):
            columns = pl.ds(group * width + head * HEAD, HEAD)
            moved = [
                back_ref[group, part, head, pl.ds(index * rows, rows), :].astype(jnp.float32)
                for part in range(ROW_SPLIT)
            ]
            here = (dq_ref, dk_ref, dv_ref)[index][:, columns]
            total = here.astype(jnp.float32) + jnp.concatenate(moved, axis=0)
            out_ref[index, :, columns] = total.astype(jnp.bfloat16)
        send(index, group).start()
    for block in blocks:
        send(*block).wait()


def add(back, arrays):
    spatial, channels = arrays[0].shape
    hbm = pl.BlockSpec(memory_space=pltpu.HBM)
    return pl.pallas_call(
        add_kernel,
        in_specs=[pl.BlockSpec(memory_space=pltpu.VMEM)] * 4,
        out_specs=[hbm] * 3,
        out_shape=[pltpu.HBM((spatial, channels), jnp.bfloat16)] * 3,
        scratch_shapes=[
            pltpu.VMEM((3, spatial, channels), jnp.bfloat16),
            pltpu.SemaphoreType.DMA((HEAD_SPLIT, 3)),
        ],
        compiler_params=pltpu.CompilerParams(vmem_limit_bytes=SCOPED),
        cost_estimate=pl.CostEstimate(
            flops=3 * spatial * channels, bytes_accessed=18 * spatial * channels, transcendentals=0
        ),
        name="add",
    )(back, *arrays)


def core_sum(sums):
    cores = [[2 * i, 2 * i + 1] for i in range(lax.axis_size("seq") // 2)]
    both = lax.all_gather(sums, "seq", axis=0, tiled=True, axis_index_groups=cores)
    return jnp.sum(both, axis=0, keepdims=True)


def ring_parts(sums, axis, stride, size):
    clips, places = lax.axis_size("dp"), lax.axis_size("seq")
    own = jnp.where(lax.rem(lax.axis_index("seq"), 2) == 0, sums, 0.0)
    if size > lax.axis_size(axis) // stride:
        return [own]

    def source(clip, place, distance):
        index = place if axis == "seq" else clip
        here = index // stride % size
        index += ((here + distance) % size - here) * stride
        return (clip, index) if axis == "seq" else (index, place)

    def receive(first, second):
        pairs = []
        for clip in range(clips):
            for place in range(places):
                distance = (first, second)[place % 2]
                if distance:
                    from_clip, from_place = source(clip, place, distance)
                    pairs.append((from_clip * places + from_place, clip * places + place))
        return lax.ppermute(sums, ("dp", "seq"), pairs)

    return [own] + [receive(first, second) for first, second in DISTANCES[size]]


def local(
    queries, key_rows, values, cotangent, frame_counts, position_counts, head_scale, frame_slope
):
    spatial, channels = queries.shape[2:]
    heads = head_scale.shape[0]
    arrays = [x.reshape(spatial, channels) for x in (queries, key_rows, values, cotangent)]
    exchange = functools.partial(
        lax.all_to_all, axis_name="seq", split_axis=0, concat_axis=0, tiled=True
    )
    packed = pack(frame_counts, position_counts, arrays)
    moved = exchange(packed)
    *space_grads, space_sum = space(frame_counts, position_counts, head_scale, arrays)
    grads, sums = time(frame_counts, head_scale, frame_slope, space_sum, moved)
    back = exchange(grads)
    sums = core_sum(sums)
    sums = core_sum(sum(ring_parts(sums, "dp", 1, 4)))
    clips = lax.axis_size("dp")
    for stride in (4, 8, 16):
        if stride < clips:
            sums = sums + lax.ppermute(sums, "dp", [(i, i ^ stride) for i in range(clips)])
    parts = ring_parts(sums, "seq", 2, 8)
    back = back.reshape((HEAD_SPLIT, ROW_SPLIT) + back.shape[1:])
    outputs = add(back, space_grads)
    outputs, parts = lax.optimization_barrier((outputs, parts))
    sums = core_sum(sum(parts))[0]
    full = queries.shape
    return tuple(x.reshape(full) for x in outputs) + (sums[:heads], sums[heads : 2 * heads])


def solution(mesh):
    split = P("dp", "seq", None, None)
    return jax.shard_map(
        local,
        mesh=mesh,
        in_specs=(split,) * 4 + (P(),) * 4,
        out_specs=(split,) * 3 + (P(),) * 2,
        check_vma=False,
    )
```

```python
import functools
import math

import jax
import jax.numpy as jnp
from jax import lax
from jax.experimental import pallas as pl
from jax.experimental.pallas import tpu as pltpu
from jax.sharding import PartitionSpec as P

HEAD = 128
ROW_SPLIT = 4
HEAD_SPLIT = 4
STEP = 8
BATCH = 7
SPACE_TYPE = jnp.bfloat16
SCOPED = 32 * 2**20
STREAM = 60 * 2**20


def dot(a, b, dims):
    return lax.dot_general(a, b, (dims, ((), ())), preferred_element_type=jnp.float32)


DISTANCES = {4: ((2, 1), (0, -1)), 8: ((4, -3), (3, -2), (0, 2), (1, -1))}

AB_T = ((1,), (1,))
AB = ((1,), (0,))
A_TB = ((0,), (0,))


def live_rows(fc_ref, pc_ref, shape):
    clip = lax.axis_index("dp")
    positions = jnp.where(lax.axis_index("seq") < fc_ref[clip], pc_ref[clip], 0)
    return lax.broadcasted_iota(jnp.int32, shape, 0) < positions


def pack_kernel(
    fc_hbm,
    pc_hbm,
    q_hbm,
    k_hbm,
    v_hbm,
    g_hbm,
    out_hbm,
    fc_ref,
    pc_ref,
    held_ref,
    out_ref,
    count_sem,
    in_sem,
    out_sem,
):
    spatial = held_ref.shape[1]
    rows = spatial // ROW_SPLIT
    heads = out_ref.shape[1]
    width = heads * HEAD

    def fetch(index, group):
        here = pl.ds(group * width, width)
        return pltpu.make_async_copy(
            (q_hbm, k_hbm, v_hbm, g_hbm)[index].at[:, here],
            held_ref.at[index, :, here],
            in_sem.at[group, index],
        )

    def send(group):
        here = pl.ds(group * ROW_SPLIT, ROW_SPLIT)
        return pltpu.make_async_copy(out_ref.at[here], out_hbm.at[here], out_sem.at[group])

    counts = (
        pltpu.make_async_copy(fc_hbm, fc_ref, count_sem.at[0]),
        pltpu.make_async_copy(pc_hbm, pc_ref, count_sem.at[1]),
    )
    for index in range(4):
        fetch(index, 0).start()
    for count in counts:
        count.start()
    for group in range(1, HEAD_SPLIT):
        for index in range(4):
            fetch(index, group).start()
    for group in range(HEAD_SPLIT):
        for index in range(4):
            fetch(index, group).wait()
            if group == 0 and index == 3:
                for count in counts:
                    count.wait()
                live = live_rows(fc_ref, pc_ref, (spatial, width))
            value = held_ref[index, :, pl.ds(group * width, width)]
            if index == 3:
                value = jnp.where(live, value, 0).astype(jnp.bfloat16)
            for part in range(ROW_SPLIT):
                for head in range(heads):
                    out_ref[group * ROW_SPLIT + part, head, pl.ds(index * rows, rows), :] = value[
                        part * rows : (part + 1) * rows, head * HEAD : (head + 1) * HEAD
                    ]
        send(group).start()
    for group in range(HEAD_SPLIT):
        send(group).wait()


def pack(frame_counts, position_counts, arrays):
    spatial, channels = arrays[0].shape
    rows = spatial // ROW_SPLIT
    hbm = pl.BlockSpec(memory_space=pltpu.HBM)
    shape = (ROW_SPLIT * HEAD_SPLIT, channels // (HEAD * HEAD_SPLIT), 4 * rows, HEAD)
    return pl.pallas_call(
        pack_kernel,
        in_specs=[hbm] * 6,
        out_specs=hbm,
        out_shape=pltpu.HBM(shape, jnp.bfloat16),
        scratch_shapes=[
            pltpu.SMEM(frame_counts.shape, jnp.int32),
            pltpu.SMEM(position_counts.shape, jnp.int32),
            pltpu.VMEM((4, spatial, channels), jnp.bfloat16),
            pltpu.VMEM(shape, jnp.bfloat16),
            pltpu.SemaphoreType.DMA((2,)),
            pltpu.SemaphoreType.DMA((HEAD_SPLIT, 4)),
            pltpu.SemaphoreType.DMA((HEAD_SPLIT,)),
        ],
        compiler_params=pltpu.CompilerParams(vmem_limit_bytes=STREAM),
        cost_estimate=pl.CostEstimate(
            flops=0, bytes_accessed=4 * 4 * spatial * channels, transcendentals=0
        ),
        name="pack",
    )(frame_counts, position_counts, *arrays)


def space_kernel(
    fc_ref, pc_ref, scale_ref, q_ref, k_ref, v_ref, g_ref, dq_ref, dk_ref, dv_ref, sum_ref
):
    head = pl.program_id(0)
    factor = scale_ref[head] * (1.0 / math.sqrt(HEAD))
    query, key, value = q_ref[...], k_ref[...], v_ref[...]
    grad = g_ref[...]
    grad = jnp.where(live_rows(fc_ref, pc_ref, grad.shape), grad, 0).astype(grad.dtype)
    raw = dot(key, query, AB_T)
    key_row = lax.broadcasted_iota(jnp.int32, raw.shape, 0)
    live = key_row < pc_ref[lax.axis_index("dp")]
    scores = jnp.where(live, raw * factor, -jnp.inf)
    exponent = jnp.exp(scores - jnp.max(scores, axis=0, keepdims=True))
    prob = exponent * (1.0 / jnp.sum(exponent, axis=0, keepdims=True))
    grad_prob = dot(value, grad, AB_T)
    weighted = prob * grad_prob
    grad_score = weighted - prob * jnp.sum(weighted, axis=0, keepdims=True)
    rounded = grad_score.astype(jnp.bfloat16)
    here = pl.ds(head * HEAD, HEAD)
    dq_ref[:, here] = (dot(rounded, key, A_TB) * factor).astype(dq_ref.dtype)
    dk_ref[:, here] = (dot(rounded, query, AB) * factor).astype(dk_ref.dtype)
    dv_ref[:, here] = dot(prob.astype(jnp.bfloat16), grad, AB).astype(dv_ref.dtype)
    term = jnp.sum(grad_score * raw) * (1.0 / math.sqrt(HEAD))
    lane = lax.broadcasted_iota(jnp.int32, sum_ref.shape, 1)

    @pl.when(head == 0)
    def _():
        sum_ref[...] = jnp.zeros_like(sum_ref)

    sum_ref[...] += jnp.where(lane == head, term, 0.0)


def space(frame_counts, position_counts, head_scale, arrays):
    spatial, channels = arrays[0].shape
    heads = channels // HEAD
    smem = pl.BlockSpec(memory_space=pltpu.SMEM)
    vmem = pl.BlockSpec(memory_space=pltpu.VMEM)
    block = pl.BlockSpec((spatial, HEAD), lambda i: (0, i))
    return pl.pallas_call(
        space_kernel,
        grid=(heads,),
        in_specs=[smem] * 3 + [block] * 4,
        out_specs=[vmem] * 3 + [pl.BlockSpec((1, HEAD), lambda i: (0, 0))],
        out_shape=[pltpu.VMEM((spatial, channels), SPACE_TYPE)] * 3
        + [jax.ShapeDtypeStruct((1, HEAD), jnp.float32)],
        compiler_params=pltpu.CompilerParams(vmem_limit_bytes=SCOPED),
        cost_estimate=pl.CostEstimate(
            flops=10 * heads * spatial * spatial * HEAD,
            bytes_accessed=20 * spatial * channels,
            transcendentals=heads * spatial * spatial,
        ),
        name="space",
    )(frame_counts, position_counts, head_scale, *arrays)


def time_kernel(
    fc_hbm,
    scale_hbm,
    slope_hbm,
    space_sum_hbm,
    moved_ref,
    out_hbm,
    sum_ref,
    fc_ref,
    scale_ref,
    slope_ref,
    space_sum_ref,
    out_ref,
    small_sem,
    out_sem,
):
    smalls = [
        pltpu.make_async_copy(source, target, small_sem.at[index])
        for index, (source, target) in enumerate(
            (
                (fc_hbm, fc_ref),
                (scale_hbm, scale_ref),
                (slope_hbm, slope_ref),
                (space_sum_hbm, space_sum_ref),
            )
        )
    ]
    for small in smalls:
        small.start()
    frames = moved_ref.shape[0]
    heads = moved_ref.shape[1]
    rows = moved_ref.shape[2] // 4
    size = frames * STEP
    steps = rows // STEP
    group = lax.div(lax.axis_index("seq"), ROW_SPLIT)
    row = lax.broadcasted_iota(jnp.int32, (size, size), 0)
    col = lax.broadcasted_iota(jnp.int32, (size, size), 1)
    row_frame, col_frame = row // STEP, col // STEP
    distance = jnp.abs(row_frame - col_frame).astype(jnp.float32)
    same = lax.rem(row, STEP) == lax.rem(col, STEP)
    sums = jnp.zeros(sum_ref.shape, jnp.float32)
    lane = lax.broadcasted_iota(jnp.int32, sums.shape, 1)
    sending = []
    for head in range(heads):
        which = group * heads + head

        def load(index, step):
            part = moved_ref[:, head, pl.ds(index * rows + step * STEP, STEP), :]
            return part.astype(jnp.float32).reshape(size, HEAD).astype(jnp.bfloat16)

        def store(index, step, value):
            value = value.reshape(frames, STEP, HEAD).astype(jnp.bfloat16)
            out_ref[:, head, pl.ds(index * rows + step * STEP, STEP), :] = value

        scale_terms = jnp.zeros((size, size), jnp.float32)
        slope_terms = jnp.zeros((size, size), jnp.float32)
        for first in range(0, steps, BATCH):
            batch = range(first, min(first + BATCH, steps))
            parts = [[load(index, step) for index in range(4)] for step in batch]
            raws = [dot(key, query, AB_T) for query, key, _, _ in parts]
            grad_probs = [dot(value, grad, AB_T) for _, _, value, grad in parts]
            if first == 0:
                if head == 0:
                    for small in smalls:
                        small.wait()
                    live = same & (row_frame < fc_ref[lax.axis_index("dp")])
                    sums = space_sum_ref[...]
                factor = scale_ref[which] * (1.0 / math.sqrt(HEAD))
                bias = jnp.where(live, -slope_ref[which] * distance, -jnp.inf)
            scores = [raw * factor + bias for raw in raws]
            exponents = [jnp.exp(x - jnp.max(x, axis=0, keepdims=True)) for x in scores]
            probs = [x * (1.0 / jnp.sum(x, axis=0, keepdims=True)) for x in exponents]
            weighted = [x * y for x, y in zip(probs, grad_probs)]
            grad_scores = [
                x - y * jnp.sum(x, axis=0, keepdims=True) for x, y in zip(weighted, probs)
            ]
            for x, raw in zip(grad_scores, raws):
                scale_terms += x * raw
                slope_terms += x
            for step, (query, key, _, grad), prob, x in zip(batch, parts, probs, grad_scores):
                rounded = x.astype(jnp.bfloat16)
                store(0, step, dot(rounded, key, A_TB) * factor)
                store(1, step, dot(rounded, query, AB) * factor)
                store(2, step, dot(prob.astype(jnp.bfloat16), grad, AB))
        sent = pltpu.make_async_copy(
            out_ref.at[:, head], out_hbm.at[:, head], out_sem.at[head]
        )
        sent.start()
        sending.append(sent)
        scale_sum = jnp.sum(scale_terms) * (1.0 / math.sqrt(HEAD))
        slope_sum = -jnp.sum(slope_terms * distance)
        sums = sums + jnp.where(lane == which, scale_sum, 0.0)
        sums = sums + jnp.where(lane == heads * HEAD_SPLIT + which, slope_sum, 0.0)
    sum_ref[...] = sums
    for sent in sending:
        sent.wait()


def time(frame_counts, head_scale, frame_slope, space_sum, moved):
    frames, heads, height, _ = moved.shape
    rows = height // 4
    hbm = pl.BlockSpec(memory_space=pltpu.HBM)
    vmem = pl.BlockSpec(memory_space=pltpu.VMEM)
    return pl.pallas_call(
        time_kernel,
        in_specs=[hbm] * 4 + [vmem],
        out_specs=[hbm, vmem],
        out_shape=[
            pltpu.HBM((frames, heads, 3 * rows, HEAD), jnp.bfloat16),
            jax.ShapeDtypeStruct((1, HEAD), jnp.float32),
        ],
        scratch_shapes=[
            pltpu.SMEM(frame_counts.shape, jnp.int32),
            pltpu.SMEM(head_scale.shape, jnp.float32),
            pltpu.SMEM(frame_slope.shape, jnp.float32),
            pltpu.VMEM(space_sum.shape, jnp.float32),
            pltpu.VMEM((frames, heads, 3 * rows, HEAD), jnp.bfloat16),
            pltpu.SemaphoreType.DMA((4,)),
            pltpu.SemaphoreType.DMA((heads,)),
        ],
        compiler_params=pltpu.CompilerParams(vmem_limit_bytes=SCOPED),
        cost_estimate=pl.CostEstimate(
            flops=10 * heads * rows * frames * frames * STEP * HEAD,
            bytes_accessed=14 * frames * rows * heads * HEAD,
            transcendentals=heads * rows * frames * frames * STEP,
        ),
        name="time",
    )(frame_counts, head_scale, frame_slope, space_sum, moved)


def add_kernel(
    back_ref, dq_ref, dk_ref, dv_ref, oq_hbm, ok_hbm, ov_hbm, out_ref, out_sem
):
    rows = dv_ref.shape[0] // ROW_SPLIT
    heads = back_ref.shape[2]
    width = heads * HEAD

    def send(index, group):
        here = pl.ds(group * width, width)
        return pltpu.make_async_copy(
            out_ref.at[index, :, here],
            (oq_hbm, ok_hbm, ov_hbm)[index].at[:, here],
            out_sem.at[group, index],
        )

    blocks = [(index, group) for index in range(3) for group in range(HEAD_SPLIT)]
    for index, group in blocks:
        for head in range(heads):
            columns = pl.ds(group * width + head * HEAD, HEAD)
            moved = [
                back_ref[group, part, head, pl.ds(index * rows, rows), :].astype(jnp.float32)
                for part in range(ROW_SPLIT)
            ]
            here = (dq_ref, dk_ref, dv_ref)[index][:, columns]
            total = here.astype(jnp.float32) + jnp.concatenate(moved, axis=0)
            out_ref[index, :, columns] = total.astype(jnp.bfloat16)
        send(index, group).start()
    for block in blocks:
        send(*block).wait()


def add(back, arrays):
    spatial, channels = arrays[0].shape
    hbm = pl.BlockSpec(memory_space=pltpu.HBM)
    return pl.pallas_call(
        add_kernel,
        in_specs=[pl.BlockSpec(memory_space=pltpu.VMEM)] * 4,
        out_specs=[hbm] * 3,
        out_shape=[pltpu.HBM((spatial, channels), jnp.bfloat16)] * 3,
        scratch_shapes=[
            pltpu.VMEM((3, spatial, channels), jnp.bfloat16),
            pltpu.SemaphoreType.DMA((HEAD_SPLIT, 3)),
        ],
        compiler_params=pltpu.CompilerParams(vmem_limit_bytes=SCOPED),
        cost_estimate=pl.CostEstimate(
            flops=3 * spatial * channels, bytes_accessed=18 * spatial * channels, transcendentals=0
        ),
        name="add",
    )(back, *arrays)


def core_sum(sums):
    cores = [[2 * i, 2 * i + 1] for i in range(lax.axis_size("seq") // 2)]
    both = lax.all_gather(sums, "seq", axis=0, tiled=True, axis_index_groups=cores)
    return jnp.sum(both, axis=0, keepdims=True)


def ring_parts(sums, axis, stride, size):
    clips, places = lax.axis_size("dp"), lax.axis_size("seq")
    own = jnp.where(lax.rem(lax.axis_index("seq"), 2) == 0, sums, 0.0)
    if size > lax.axis_size(axis) // stride:
        return [own]

    def source(clip, place, distance):
        index = place if axis == "seq" else clip
        here = index // stride % size
        index += ((here + distance) % size - here) * stride
        return (clip, index) if axis == "seq" else (index, place)

    def receive(first, second):
        pairs = []
        for clip in range(clips):
            for place in range(places):
                distance = (first, second)[place % 2]
                if distance:
                    from_clip, from_place = source(clip, place, distance)
                    pairs.append((from_clip * places + from_place, clip * places + place))
        return lax.ppermute(sums, ("dp", "seq"), pairs)

    return [own] + [receive(first, second) for first, second in DISTANCES[size]]


def local(
    queries, key_rows, values, cotangent, frame_counts, position_counts, head_scale, frame_slope
):
    spatial, channels = queries.shape[2:]
    heads = head_scale.shape[0]
    arrays = [x.reshape(spatial, channels) for x in (queries, key_rows, values, cotangent)]
    exchange = functools.partial(
        lax.all_to_all, axis_name="seq", split_axis=0, concat_axis=0, tiled=True
    )
    packed = pack(frame_counts, position_counts, arrays)
    moved = exchange(packed)
    *space_grads, space_sum = space(frame_counts, position_counts, head_scale, arrays)
    grads, sums = time(frame_counts, head_scale, frame_slope, space_sum, moved)
    back = exchange(grads)
    sums = core_sum(sums)
    sums = core_sum(sum(ring_parts(sums, "dp", 1, 4)))
    clips = lax.axis_size("dp")
    for stride in (16, 8, 4):
        if stride < clips:
            sums = sums + lax.ppermute(sums, "dp", [(i, i ^ stride) for i in range(clips)])
    parts = ring_parts(sums, "seq", 2, 8)
    back = back.reshape((HEAD_SPLIT, ROW_SPLIT) + back.shape[1:])
    outputs = add(back, space_grads)
    outputs, parts = lax.optimization_barrier((outputs, parts))
    sums = core_sum(sum(parts))[0]
    full = queries.shape
    return tuple(x.reshape(full) for x in outputs) + (sums[:heads], sums[heads : 2 * heads])


def solution(mesh):
    split = P("dp", "seq", None, None)
    return jax.shard_map(
        local,
        mesh=mesh,
        in_specs=(split,) * 4 + (P(),) * 4,
        out_specs=(split,) * 3 + (P(),) * 2,
        check_vma=False,
    )
```
